256 devices in a mesh: lon: 16 (over z, y_hi), lat: 8 (over x, y_lo), lev: 2 (over core).
Axes of the slice: x: 4, y: 4 (y_hi: 2, y_lo: 2; y = y_hi * 2 + y_lo), z: 8, core: 2. Of those that a mesh axis runs over, the one named last changes fastest.
Arguments:
- tokens: bfloat16 [8, 16, 256, 512], P('lev', 'lat', 'lon'), may hold values from -6 to 6
- w_qkv: bfloat16 [512, 1536], replicated
- w_out: bfloat16 [512, 512], replicated, may hold values from -0.25 to 0.25
- w_up: bfloat16 [512, 2048], replicated, may hold values from -0.25 to 0.25
- w_down: bfloat16 [2048, 512], replicated, may hold values from -0.125 to 0.125
- tile_mask: int32 [8, 16, 5], P('lat', 'lon'), may hold values 0 or 1
- level_group: int32 [8], replicated, may hold values from 0 to 1
- row_shift: int32 [16], P('lat'), may hold values from -24 to 24, as said below
Outputs:
- updated: bfloat16 [8, 16, 256, 512], P('lev', 'lat', 'lon')
The draws below stay inside these ranges and needn't reach their ends.
Inputs may be any that keep to these rules, and one draw needn't show every extreme that they name: `row_shift`: each of the two extremes is taken by some row.
All inputs are finite; a program needn't handle non-finite values. No bound on the sum of `tile_mask` on one device may be relied on, other than what follows from the above.
Results may differ from the reference program's by a relative error of at most 0.0065.
Values may be sent and summed in bfloat16 or wider, within the bound.
A program may use at most 64 MiB of HBM per device.

```python
import jax
import jax.numpy as jnp
from jax import lax

D = 512
HEADS = 16
HEAD_DIM = 32
FF = 2048
CLAT = 2
CLON = 16
OFFSETS = 5
LEV = 8
LAT = 16
LON = 256
BANDS = 8
TILES = 16
N_LON = 16
N_LAT = 8


def draw_row_shift(key, part):
    key = jax.random.fold_in(key, 5)
    reach = CLON + CLON // 2
    first, second = jax.random.split(key)
    values = jax.random.randint(first, (LAT,), -reach, reach + 1).astype(jnp.int32)
    order = jax.random.permutation(second, LAT)
    values = values.at[order[0]].set(reach)
    return values.at[order[1]].set(-reach).astype(jnp.int32)


def draw_w_qkv(key, part):
    key = jax.random.fold_in(key, 9)
    first = jax.random.fold_in(key, 0)
    base = jax.random.normal(first, (D, 3 * D), jnp.float32) * D ** (-0.5)
    return base.astype(jnp.bfloat16)


def touch_ends(drawn, rng, smallest, largest):
    place = [jax.random.randint(jax.random.fold_in(rng, axis), (), 0, length) for axis, length in enumerate(drawn.shape)]
    longest = drawn.shape.index(max(drawn.shape))
    beside = place[:longest] + [(place[longest] + 1) % drawn.shape[longest]] + place[longest + 1:]
    return drawn.at[tuple(place)].set(smallest).at[tuple(beside)].set(largest)


def level_of(rng, dims, shards, smallest, top_value):
    gain = 1.0
    for position, parts in shards:
        heights = jax.random.uniform(jax.random.fold_in(jax.random.fold_in(rng, 6), position), (parts,), jnp.float32, smallest / len(shards), top_value / len(shards))
        gain = gain * jnp.repeat(jnp.exp(heights), dims[position] // parts).reshape((-1,) + (1,) * (len(dims) - 1 - position))
    return gain


def bell_draw(own_key, extent, scale, bound, cuts=(), held_as=jnp.bfloat16):
    level = level_of(own_key, extent, cuts, -0.22, 0.18) if cuts else 1.0
    values = jax.random.normal(own_key, extent, jnp.float32) * scale * level
    return jnp.minimum(jnp.maximum(values, -bound), bound).astype(held_as)


def setup_inputs(seed: int = 0) -> dict:
    arg_keys = jax.random.split(jax.random.key(seed), 9)
    tokens = bell_draw(arg_keys[0], (LEV, LAT, LON, D), 1.0, 6.0, ((0, 2), (1, 8), (2, 16)))
    w_qkv = draw_w_qkv(jax.random.fold_in(arg_keys[8], 71), 0)
    w_out = bell_draw(arg_keys[2], (D, D), D ** -0.5, 0.25)
    w_up = bell_draw(arg_keys[3], (D, FF), D ** -0.5, 0.25)
    w_down = bell_draw(arg_keys[4], (FF, D), FF ** -0.5, 0.125)
    tile_mask = touch_ends((jax.random.randint(arg_keys[5], (BANDS, TILES, OFFSETS), 0, 2) < 1).astype(jnp.int32), jax.random.fold_in(arg_keys[5], 1), 0, 1)
    level_group = touch_ends(jax.random.randint(arg_keys[6], (LEV,), 0, 2), jax.random.fold_in(arg_keys[6], 1), 0, 1).astype(jnp.int32)
    row_shift = draw_row_shift(jax.random.fold_in(arg_keys[8], 71), 0)
    return {"tokens": tokens, "w_qkv": w_qkv, "w_out": w_out, "w_up": w_up, "w_down": w_down, "tile_mask": tile_mask, "level_group": level_group, "row_shift": row_shift}


def normalize(values):
    centred = values - lax.optimization_barrier(jnp.mean(values, axis=-1, keepdims=True))
    spread = lax.optimization_barrier(jnp.mean(centred * centred, axis=-1, keepdims=True))
    return centred * lax.rsqrt(spread + 1e-05)

def reference(tokens, w_qkv, w_out, w_up, w_down, tile_mask, level_group, row_shift):
    inputs = tokens.astype(jnp.float32).reshape(-1, D)
    normed = normalize(inputs).astype(jnp.bfloat16)
    projected = jnp.dot(normed, w_qkv, preferred_element_type=jnp.float32)
    queries = (projected[:, :D] * HEAD_DIM ** (-0.5)).astype(jnp.bfloat16).reshape(LEV, LAT, LON, D)
    keyvals = projected[:, D:].astype(jnp.bfloat16).reshape(LEV, LAT, LON, 2 * D)
    padded = jnp.pad(keyvals, ((0, 0), (1, 1), (0, 0), (0, 0)))
    same_group = level_group[:, None] == level_group[None, :]
    offsets = jnp.arange(-2 * CLON, 3 * CLON)
    distance = offsets[None, :] - jnp.arange(CLON)[:, None]
    half = CLON // 2

    def one_tile(index):
        band = (index // N_LON).astype(jnp.int32)
        column = (index % N_LON).astype(jnp.int32)
        anchor = jnp.zeros((), jnp.int32)
        tile_queries = lax.dynamic_slice(queries, (anchor, band * CLAT, column * CLON, anchor), (LEV, CLAT, CLON, D))
        tile_queries = tile_queries.reshape(-1, HEADS, HEAD_DIM).astype(jnp.float32)
        band_rows = lax.dynamic_slice_in_dim(padded, band * CLAT, CLAT + 2, 1)
        picked = (column * CLON + offsets) % LON
        window = jnp.take(band_rows, picked, axis=2).reshape(-1, 2 * D)
        keys = window[:, :D].reshape(-1, HEADS, HEAD_DIM).astype(jnp.float32)
        values = window[:, D:].reshape(-1, HEADS, HEAD_DIM).astype(jnp.float32)
        query_row = band * CLAT + jnp.arange(CLAT)
        key_row = band * CLAT - 1 + jnp.arange(CLAT + 2)
        row_ok = (jnp.abs(key_row[None, :] - query_row[:, None]) <= 1) & (key_row >= 0)[None, :] & (key_row < LAT)[None, :]
        shifts = lax.dynamic_slice_in_dim(row_shift, band * CLAT, CLAT)
        col_ok = (jnp.abs(distance) <= half)[None, :, :] | (jnp.abs(distance[None, :, :] - shifts[:, None, None]) <= half)
        allowed = (tile_mask[band, column] > 0) | (jnp.arange(OFFSETS) == OFFSETS // 2)
        tile_ok = jnp.repeat(allowed, CLON)
        visible = same_group[:, None, None, :, None, None] & row_ok[None, :, None, None, :, None] & col_ok[None, :, :, None, None, :] & tile_ok
        visible = visible.reshape(LEV * CLAT * CLON, -1)
        scores = jnp.einsum('qhd,khd->hqk', tile_queries, keys)
        scores = jnp.where(visible[None], scores, -jnp.inf)
        highest = lax.optimization_barrier(jnp.max(scores, axis=-1, keepdims=True))
        weights = jnp.exp(scores - highest)
        total = lax.optimization_barrier(jnp.sum(weights, axis=-1))
        probs = weights.astype(jnp.bfloat16).astype(jnp.float32)
        weighted = jnp.einsum('hqk,khd->qhd', probs, values)
        result = weighted / jnp.transpose(total)[:, :, None]
        return result.astype(jnp.bfloat16).reshape(LEV, CLAT, CLON, D)
    tiles = lax.map(one_tile, jnp.arange(N_LAT * N_LON, dtype=jnp.int32))
    attended = tiles.reshape(N_LAT, N_LON, LEV, CLAT, CLON, D).transpose(2, 0, 3, 1, 4, 5).reshape(-1, D)
    middle = inputs + jnp.dot(attended, w_out, preferred_element_type=jnp.float32)
    mid_normed = normalize(middle).astype(jnp.bfloat16)
    hidden = jax.nn.gelu(jnp.dot(mid_normed, w_up, preferred_element_type=jnp.float32), approximate=False).astype(jnp.bfloat16)
    updated = middle + jnp.dot(hidden, w_down, preferred_element_type=jnp.float32)
    return updated.astype(jnp.bfloat16).reshape(LEV, LAT, LON, D)
```

```python
import functools

import jax
import jax.numpy as jnp
from jax import lax
from jax.experimental import pallas as pl
from jax.experimental.pallas import tpu as pltpu
from jax.sharding import PartitionSpec as P

WIDTH = 512
HALF = 256
HEAD_DIM = 32
FF = 2048
EMPTY = -1e30
TINY = 1e-30
F32 = jnp.float32
BF16 = jnp.bfloat16
MESH = pl.DeviceIdType.MESH

M_PARTNER = 0
M_LOP = 2
M_XN = 3
M_PLOP = 4
M_PXN = 5
M_FAR = 6
M_OPP = 8
M_NEAR = 12
M_FAR_LOP = 14
M_FAR_XN = 15
M_OPP_PLOP = 16
M_OPP_PXN = 17
M_SIB = 18
M_PART = 20
M_WRAP = 22
M_OPP_LOP = 24
M_OPP_XN = 25
MESSAGES = 26


def normalize(values):
    centred = values - jnp.mean(values, axis=-1, keepdims=True)
    spread = jnp.mean(centred * centred, axis=-1, keepdims=True)
    return centred * lax.rsqrt(spread + 1e-05)


def kernel(
    tokens, w_qkv, w_out, w_up, w_down, tile_mask_h, level_group_h, row_shift_h, out,
    tile_mask, level_group, row_shift, win, sib, v_qkv, v_out, v_up, v_down, kv, queries, bias,
    bias_far, keep_o, keep_m,
    keep_l, part, got, send, recv, local, ready,
):
    lon, lat, lev = (lax.axis_index(a) for a in ("lon", "lat", "lev"))
    odd_lon, odd_lat = lax.rem(lon, 2), lax.rem(lat, 2)
    sigma, tau = 1 - 2 * odd_lon, 1 - 2 * odd_lat
    partner = lon + sigma
    lop = lat + tau
    xn = lax.rem(lat - tau + 8, 8)
    has_xn = (lat > 0) & (lat < 7)
    no_xn = (lat == 0) | (lat == 7)
    depth = lon // 2
    up, down = lax.rem(lon + 2, 16), lax.rem(lon + 14, 16)
    zp = lax.rem(lon + 2 * sigma + 16, 16)
    zm = lax.rem(lon - 2 * sigma + 16, 16)
    other = 1 - lev
    far, opp = 3 + odd_lon, 4 - odd_lon
    prow, xrow = 3 * (1 - odd_lat), 3 * odd_lat

    def device(lo=None, la=None, le=None):
        return (lon if lo is None else lo, lat if la is None else la, lev if le is None else le)

    last = depth == 7
    first = depth == 0
    wraps = lon == 15
    wrapped, wrapped_edges = lon == 0, lon == 1
    sends_near = (depth < 7) | (odd_lon == 1)
    sends_edges = (depth < 7) | (odd_lon == 0)
    takes_near = (depth > 0) | (odd_lon == 1)
    takes_edges = (depth > 0) | (odd_lon == 0)
    barrier = pltpu.get_barrier_semaphore()

    def greet(peer):
        pl.semaphore_signal(barrier, inc=1, device_id=peer, device_id_type=MESH)

    even_lon, even_lat = odd_lon == 0, odd_lat == 0
    beside = [
        (device(lo=partner), even_lon, None),
        (device(la=lop), even_lat, None),
        (device(la=xn), odd_lat == 1, has_xn),
        (device(lo=partner, la=lop), even_lon, None),
        (device(lo=partner, la=xn), even_lon, has_xn),
        (device(le=other), lev == 0, None),
    ]
    greetings = jnp.where(first, 0, 1) + jnp.where(last, 1, 0)
    for peer, greets, exists in beside:
        greetings += jnp.where(greets, 0, 1 if exists is None else jnp.where(exists, 1, 0))

        @pl.when(greets if exists is None else greets & exists)
        def _():
            greet(peer)

    @pl.when(depth < 7)
    def _():
        greet(device(lo=up))

    @pl.when(first)
    def _():
        greet(device(lo=down))

    @pl.when(wrapped)
    def _():
        greet(device(lo=15))

    loads = []
    for r in range(2):
        loads.append(pltpu.make_async_copy(tokens.at[:, r], win.at[0, 1 + r], local.at[r]))
    loads.append(pltpu.make_async_copy(w_qkv, v_qkv, local.at[2]))
    loads.append(pltpu.make_async_copy(w_out, v_out, local.at[3]))
    loads.append(pltpu.make_async_copy(w_up, v_up, local.at[4]))
    loads.append(pltpu.make_async_copy(w_down, v_down, local.at[5]))
    for load in loads:
        load.start()
    tables = [
        pltpu.make_async_copy(tile_mask_h, tile_mask, local.at[6]),
        pltpu.make_async_copy(level_group_h, level_group, local.at[7]),
        pltpu.make_async_copy(row_shift_h, row_shift, local.at[8]),
    ]
    for table in tables:
        table.start()

    greetings += jnp.where(wraps, 1, 0)
    @pl.when(greetings > 0)
    def _():
        pl.semaphore_wait(barrier, greetings)

    for number, (peer, greets, exists) in enumerate(beside):
        answers = jnp.logical_not(greets)

        @pl.when(answers if exists is None else answers & exists)
        def _():
            pl.semaphore_signal(ready.at[2 + number], inc=1, device_id=peer, device_id_type=MESH)

    def await_peer(*numbers):
        for number in numbers:
            _, greets, exists = beside[number]

            @pl.when(greets if exists is None else greets & exists)
            def _():
                pl.semaphore_wait(ready.at[2 + number], 1)

    @pl.when(depth > 0)
    def _():
        pl.semaphore_signal(ready.at[0], inc=1, device_id=device(lo=down), device_id_type=MESH)

    @pl.when(last)
    def _():
        pl.semaphore_signal(ready.at[1], inc=1, device_id=device(lo=up), device_id_type=MESH)

    up_row, down_row = 1 - odd_lat, odd_lat
    lop_at, xn_at = 3 * odd_lat, 3 * (1 - odd_lat)
    routes = {
        M_LOP: (tokens.at[:, up_row], win.at[0, lop_at], device(la=lop)),
        M_XN: (tokens.at[:, down_row], win.at[0, xn_at], device(la=xn)),
        M_PLOP: (tokens.at[:, up_row], win.at[1, lop_at], device(lo=partner, la=lop)),
        M_PXN: (tokens.at[:, down_row], win.at[1, xn_at], device(lo=partner, la=xn)),
        M_OPP + 2: (win.at[0, prow], win.at[opp, prow], device(lo=zm)),
        M_OPP + 3: (win.at[0, xrow], win.at[opp, xrow], device(lo=zm)),
        M_FAR_LOP: (win.at[far, 1 + up_row], win.at[far, lop_at], device(la=lop)),
        M_FAR_XN: (win.at[far, 1 + down_row], win.at[far, xn_at], device(la=xn)),
        M_OPP_LOP: (win.at[opp, 1 + up_row], win.at[opp, lop_at], device(la=lop)),
        M_OPP_XN: (win.at[opp, 1 + down_row], win.at[opp, xn_at], device(la=xn)),
        M_OPP_PLOP: (
            win.at[opp, 1 + up_row], win.at[2, lop_at], device(lo=partner, la=lop)),
        M_OPP_PXN: (
            win.at[opp, 1 + down_row], win.at[2, xn_at], device(lo=partner, la=xn)),
    }
    for r in range(2):
        routes[M_PARTNER + r] = (tokens.at[:, r], win.at[1, 1 + r], device(lo=partner))
        routes[M_FAR + r] = (tokens.at[:, r], win.at[far, 1 + r], device(lo=zp))
        routes[M_OPP + r] = (tokens.at[:, r], win.at[opp, 1 + r], device(lo=zm))
        routes[M_NEAR + r] = (win.at[1, 1 + r], win.at[2, 1 + r], device(lo=zp))
        routes[M_WRAP + r] = (tokens.at[:, r], win.at[2, 1 + r], device(lo=0))
        routes[M_SIB + r] = (tokens.at[:, r], sib.at[r], device(le=other))
        routes[M_PART + r] = (part.at[r], got.at[r], device(le=other))
    def message(number):
        src, dst, peer = routes[number]
        return pltpu.make_async_remote_copy(
            src_ref=src, dst_ref=dst, send_sem=send.at[number], recv_sem=recv.at[number],
            device_id=peer, device_id_type=MESH,
        )

    def begin(*numbers):
        for number in numbers:
            message(number).start()

    def arrived(*numbers):
        for number in numbers:
            message(number).wait_recv()

    zp_step = jnp.where(odd_lon == 0, jnp.where(last, 0, 1), jnp.where(first, 2, 0))
    zm_step = jnp.where(odd_lon == 1, jnp.where(last, 0, 1), jnp.where(first, 2, 0))

    def begin_z(step):
        @pl.when(zp_step == step)
        def _():
            begin(M_FAR, M_FAR + 1)

        @pl.when(zm_step == step)
        def _():
            begin(M_OPP, M_OPP + 1)

    begin_z(0)

    @pl.when(wraps)
    def _():
        begin(M_WRAP, M_WRAP + 1)

    await_peer(0)
    begin(M_PARTNER, M_PARTNER + 1)
    await_peer(5)
    begin(M_SIB, M_SIB + 1)

    @pl.when(depth < 7)
    def _():
        pl.semaphore_wait(ready.at[0], 1)

    begin_z(1)
    await_peer(1, 3, 2, 4)
    begin(M_LOP, M_PLOP)

    @pl.when(has_xn)
    def _():
        begin(M_XN, M_PXN)

    @pl.when(no_xn)
    def _():
        for slot in range(5):
            win[slot, xrow] = jnp.zeros((4, 16, WIDTH), BF16)

    def project_queries(owner, rows):
        normed = normalize(rows.astype(F32)).astype(BF16)
        q = jnp.dot(normed, v_qkv[:, :WIDTH], preferred_element_type=F32) * HEAD_DIM ** (-0.5)
        queries[owner] = q.astype(BF16).reshape(2, 64, WIDTH)

    def project_keys(places):
        rows = jnp.concatenate(
            [win[slot, row].reshape(64, WIDTH) for slot, row in places], axis=0)
        normed = normalize(rows.astype(F32)).astype(BF16)
        both = jnp.dot(normed, v_qkv[:, WIDTH:], preferred_element_type=F32).astype(BF16)
        for i, (slot, row) in enumerate(places):
            kv[slot, row] = both[64 * i:64 * (i + 1)]

    for load in loads[:3]:
        load.wait()
    project_queries(1, win[0, 1:3].reshape(128, WIDTH))

    project_keys([(0, 1), (0, 2)])

    for table in tables:
        table.wait()

    def iota(shape, dim):
        return lax.broadcasted_iota(jnp.int32, shape, dim)

    def spread(at, starts, values):
        result = jnp.full(at.shape, values[0], jnp.int32)
        for start, value in zip(starts[1:], values[1:]):
            result = jnp.where(at >= start, value, result)
        return result

    own_at = iota((64, 1), 0)
    q_col = own_at & 15
    q_lev = lax.shift_right_logical(own_at, 4)

    def pick(index, values):
        result = jnp.full(index.shape, values[0], jnp.int32)
        for i in range(1, len(values)):
            result = jnp.where(index == i, values[i], result)
        return result

    own_groups = [level_group[lev * 4 + i] for i in range(4)]
    q_groups = [
        pick(q_lev, [level_group[whose * 4 + i] for i in range(4)]) for whose in (other, lev)]
    dyn_slot = []
    for r in range(2):
        shift = row_shift[r]
        right = shift > 0
        dyn_slot.append(jnp.where(right, 4, 3))
        dyn_offset = jnp.where(right, 2, -2)
        dyn_ok = jnp.where(right, tile_mask[0, 0, 4], tile_mask[0, 0, 0])
        west, east = tile_mask[0, 0, 1], tile_mask[0, 0, 3]
        near_ok = jnp.where(odd_lon == 0, west, east)
        partner_ok = jnp.where(odd_lon == 0, east, west)
        edge = 3 * r
        for mask, starts, first_rows, offsets, tiles in (
            (bias, (0, 192, 384), (r, r, 1), (0, sigma, dyn_offset), (1, partner_ok, dyn_ok)),
            (bias_far, (0, 192), (r, edge), (-sigma, dyn_offset), (near_ok, dyn_ok)),
        ):
            at = iota((1, mask.shape[-1]), 1)
            in_segment = at - spread(at, starts, starts)
            key_row = lax.shift_right_logical(in_segment, 6) + spread(at, starts, first_rows)
            key_lev = lax.shift_right_logical(in_segment & 63, 4)
            key_col = in_segment & 15
            absolute = lat * 2 - 1 + key_row
            row_ok = (absolute >= 0) & (absolute < 16)
            offset = spread(at, starts, offsets)
            tile_ok = spread(at, starts, tiles)
            distance = offset * 16 + key_col - q_col
            near = (jnp.abs(distance) <= 8) | (jnp.abs(distance - shift) <= 8)
            near = near & (row_ok & (tile_ok > 0))
            key_group = pick(key_lev, own_groups)
            for owner in range(2):
                visible = near & (q_groups[owner] == key_group)
                mask[owner, r] = jnp.where(visible, 0.0, -jnp.inf).astype(F32)

    def forward_near(r):
        @pl.when(sends_near)
        def _():
            begin(M_NEAR + r)

    def forward_edges():
        @pl.when(sends_edges)
        def _():
            begin(M_OPP + 2)

            @pl.when(has_xn)
            def _():
                begin(M_OPP + 3)

    def forward_far():
        arrived(M_FAR, M_FAR + 1)
        begin(M_FAR_LOP)

        @pl.when(has_xn)
        def _():
            begin(M_FAR_XN)

    def forward_opp():
        arrived(M_OPP, M_OPP + 1)

        @pl.when(wrapped_edges)
        def _():
            begin(M_OPP_LOP)

            @pl.when(has_xn)
            def _():
                begin(M_OPP_XN)

        begin(M_OPP_PLOP)

        @pl.when(has_xn)
        def _():
            begin(M_OPP_PXN)

    def project_far():
        project_keys([(slot, row) for slot in (3, 4) for row in (1, 2)])

    arrived(M_PARTNER)

    @pl.when(first)
    def _():
        pl.semaphore_wait(ready.at[1], 1)

    begin_z(2)
    forward_near(0)
    arrived(M_PARTNER + 1)
    forward_near(1)
    arrived(M_LOP)

    @pl.when(has_xn)
    def _():
        arrived(M_XN)

    forward_edges()
    arrived(M_SIB, M_SIB + 1)
    project_queries(0, sib[...].reshape(128, WIDTH))

    pl.when(lon != 0)(forward_far)
    pl.when(lon != 1)(forward_opp)
    pl.when(depth > 0)(project_far)

    pl.when(lon == 0)(forward_far)
    pl.when(lon == 1)(forward_opp)
    arrived(M_PLOP)

    @pl.when(has_xn)
    def _():
        arrived(M_PXN)

    project_keys([(1, row) for row in range(4)] + [(0, 0), (0, 3)])


    pl.when(first)(project_far)

    lane_head = lax.shift_right_logical(iota((1, HALF), 1), 5)
    head_is = [lane_head == h for h in range(8)]
    head_one = [h.astype(F32).astype(BF16) for h in head_is]

    def attend(owner, r, half, phase, mask):
        lower = half * HALF
        q = queries[owner, r, :, lower:lower + HALF]
        stacked = jnp.concatenate([q * head_one[h] for h in range(8)], axis=0)
        pieces = [(dyn_slot[r], slice(1, 3) if phase == 0 else slice(3 * r, 3 * r + 1))]
        pieces = [(slot, slice(r, r + 3)) for slot in ((0, 1) if phase == 0 else (2,))] + pieces
        k, v = (
            jnp.concatenate([
                kv[slot, rows, :, start:start + HALF].reshape(-1, HALF) for slot, rows in pieces
            ], axis=0)
            for start in (lower, WIDTH + lower)
        )
        scores = lax.dot_general(
            stacked, k, (((1,), (1,)), ((), ())), preferred_element_type=F32)
        scores = scores.reshape(8, 64, -1) + mask[owner, r][None]
        highest = jnp.maximum(jnp.max(scores, axis=-1, keepdims=True), EMPTY)
        weights = jnp.exp(scores - highest)
        total = jnp.sum(weights, axis=-1, keepdims=True)
        probs = weights.astype(BF16).reshape(512, -1)
        summed = jnp.dot(probs, v, preferred_element_type=F32).reshape(8, 64, HALF)
        o, m, l = summed[0], highest[0], total[0]
        for h in range(1, 8):
            o = jnp.where(head_is[h], summed[h], o)
            m = jnp.where(head_is[h], highest[h], m)
            l = jnp.where(head_is[h], total[h], l)
        return o, m, l

    for owner in range(2):
        for r in range(2):
            for half in range(2):
                o, m, l = attend(owner, r, half, 0, bias)
                at = (owner, r, slice(None), slice(half * HALF, (half + 1) * HALF))
                keep_o[at], keep_m[at], keep_l[at] = o, m, l

    @pl.when(takes_near)
    def _():
        arrived(M_NEAR, M_NEAR + 1)

    @pl.when(wrapped)
    def _():
        arrived(M_WRAP, M_WRAP + 1)

    project_keys([(2, 1), (2, 2)])

    def merged(owner, r, half, phase, mask):
        o, m, l = attend(owner, r, half, phase, mask)
        at = (owner, r, slice(None), slice(half * HALF, (half + 1) * HALF))
        top = jnp.maximum(m, keep_m[at])
        old, new = jnp.exp(keep_m[at] - top), jnp.exp(m - top)
        return at, old * keep_o[at] + new * o, top, old * keep_l[at] + new * l

    @pl.when(takes_edges)
    def _():
        arrived(M_OPP + 2)

        @pl.when(has_xn)
        def _():
            arrived(M_OPP + 3)

    @pl.when(wrapped_edges)
    def _():
        arrived(M_OPP_LOP)

        @pl.when(has_xn)
        def _():
            arrived(M_OPP_XN)

    arrived(M_FAR_LOP, M_OPP_PLOP)

    @pl.when(has_xn)
    def _():
        arrived(M_FAR_XN, M_OPP_PXN)

    project_keys([(slot, row) for slot in (2, 3, 4) for row in (0, 3)])

    for owner in range(2):
        for r in range(2):
            for half in range(2):
                at, o, top, l = merged(owner, r, half, 1, bias_far)
                l = jnp.maximum(l, TINY)
                if owner == 0:
                    part[r, 0, :, at[-1]] = o / l
                    part[r, 1, :, at[-1]] = top + jnp.log(l)
                else:
                    keep_o[at], keep_m[at] = o / l, top + jnp.log(l)
            if owner == 0:
                begin(M_PART + r)

    rows = []
    for r in range(2):
        arrived(M_PART + r)
        mine, theirs = keep_m[1, r], got[r, 1]
        top = jnp.maximum(mine, theirs)
        mine, theirs = jnp.exp(mine - top), jnp.exp(theirs - top)
        rows.append((mine * keep_o[1, r] + theirs * got[r, 0]) / (mine + theirs))
    attended = jnp.concatenate(rows, axis=0).astype(BF16)

    for load in loads[3:]:
        load.wait()
    inputs = win[0, 1:3].reshape(128, WIDTH).astype(F32)
    middle = inputs + jnp.dot(attended, v_out[...], preferred_element_type=F32)
    mid_normed = normalize(middle).astype(BF16)
    updated = middle
    for start in range(0, FF, 512):
        hidden = jnp.dot(mid_normed, v_up[:, start:start + 512], preferred_element_type=F32)
        hidden = 0.5 * hidden * (1.0 + lax.erf(hidden * 0.5 ** 0.5))
        updated = updated + jnp.dot(
            hidden.astype(BF16), v_down[start:start + 512, :], preferred_element_type=F32)
    updated = updated.astype(BF16).reshape(2, 4, 16, WIDTH)
    for r in range(2):
        out[:, r] = updated[r]

    def sent(*numbers):
        for number in numbers:
            message(number).wait_send()

    sent(*range(M_PARTNER, M_PARTNER + 2), M_LOP, M_PLOP, M_FAR, M_FAR + 1, M_OPP, M_OPP + 1)
    sent(M_FAR_LOP, M_OPP_PLOP, M_SIB, M_SIB + 1, M_PART, M_PART + 1)

    @pl.when(has_xn)
    def _():
        sent(M_XN, M_PXN, M_FAR_XN, M_OPP_PXN)

    @pl.when(sends_near)
    def _():
        sent(M_NEAR, M_NEAR + 1)

    @pl.when(sends_edges)
    def _():
        sent(M_OPP + 2)

        @pl.when(has_xn)
        def _():
            sent(M_OPP + 3)

    @pl.when(wraps)
    def _():
        sent(M_WRAP, M_WRAP + 1)

    @pl.when(wrapped_edges)
    def _():
        sent(M_OPP_LOP)

        @pl.when(has_xn)
        def _():
            sent(M_OPP_XN)


def on_device(tokens, w_qkv, w_out, w_up, w_down, tile_mask, level_group, row_shift):
    anywhere = pl.BlockSpec(memory_space=pltpu.HBM)
    vmem = pltpu.VMEM
    return pl.pallas_call(
        kernel,
        out_shape=vmem(tokens.shape, BF16),
        in_specs=[anywhere] * 8,
        out_specs=pl.BlockSpec(memory_space=pltpu.VMEM),
        scratch_shapes=[
            pltpu.SMEM((1, 1, 5), jnp.int32),
            pltpu.SMEM((8,), jnp.int32),
            pltpu.SMEM((2,), jnp.int32),
            vmem((5, 4, 4, 16, WIDTH), BF16),
            vmem((2, 4, 16, WIDTH), BF16),
            vmem((WIDTH, 3 * WIDTH), BF16),
            vmem((WIDTH, WIDTH), BF16),
            vmem((WIDTH, FF), BF16),
            vmem((FF, WIDTH), BF16),
            vmem((5, 4, 64, 2 * WIDTH), BF16),
            vmem((2, 2, 64, WIDTH), BF16),
            vmem((2, 2, 64, 512), F32),
            vmem((2, 2, 64, 256), F32),
            vmem((2, 2, 64, WIDTH), F32),
            vmem((2, 2, 64, WIDTH), F32),
            vmem((2, 2, 64, WIDTH), F32),
            vmem((2, 2, 64, WIDTH), F32),
            vmem((2, 2, 64, WIDTH), F32),
            pltpu.SemaphoreType.DMA((MESSAGES,)),
            pltpu.SemaphoreType.DMA((MESSAGES,)),
            pltpu.SemaphoreType.DMA((9,)),
            pltpu.SemaphoreType.REGULAR((8,)),
        ],
        compiler_params=pltpu.CompilerParams(
            collective_id=0, has_side_effects=True, vmem_limit_bytes=60 * 1024 * 1024),
        cost_estimate=pl.CostEstimate(
            flops=6 * 10 ** 9, bytes_accessed=7 * 10 ** 6, transcendentals=4 * 10 ** 6),
    )(tokens, w_qkv, w_out, w_up, w_down, tile_mask, level_group, row_shift)


def solution(mesh):
    placed = (
        P("lev", "lat", "lon", None), P(), P(), P(), P(), P("lat", "lon", None), P(), P("lat"),
    )
    return jax.shard_map(
        on_device, mesh=mesh, in_specs=placed, out_specs=P("lev", "lat", "lon", None),
        check_vma=False,
    )
```

```python
import functools

import jax
import jax.numpy as jnp
from jax import lax
from jax.experimental import pallas as pl
from jax.experimental.pallas import tpu as pltpu
from jax.sharding import PartitionSpec as P

WIDTH = 512
HALF = 256
HEAD_DIM = 32
FF = 2048
EMPTY = -1e30
TINY = 1e-30
F32 = jnp.float32
BF16 = jnp.bfloat16
MESH = pl.DeviceIdType.MESH

M_PARTNER = 0
M_LOP = 2
M_XN = 3
M_PLOP = 4
M_PXN = 5
M_FAR = 6
M_OPP = 8
M_NEAR = 12
M_FAR_LOP = 14
M_FAR_XN = 15
M_OPP_PLOP = 16
M_OPP_PXN = 17
M_SIB = 18
M_PART = 20
M_WRAP = 22
M_OPP_LOP = 24
M_OPP_XN = 25
MESSAGES = 26


def normalize(values):
    centred = values - jnp.mean(values, axis=-1, keepdims=True)
    spread = jnp.mean(centred * centred, axis=-1, keepdims=True)
    return centred * lax.rsqrt(spread + 1e-05)


def kernel(
    tokens, w_qkv, w_out, w_up, w_down, tile_mask_h, level_group_h, row_shift_h, out,
    tile_mask, level_group, row_shift, win, sib, v_qkv, v_out, v_up, v_down, kv, kv_edge, queries, bias,
    bias_far, keep_o, keep_m,
    keep_l, part, got, send, recv, local, ready,
):
    lon, lat, lev = (lax.axis_index(a) for a in ("lon", "lat", "lev"))
    odd_lon, odd_lat = lax.rem(lon, 2), lax.rem(lat, 2)
    sigma, tau = 1 - 2 * odd_lon, 1 - 2 * odd_lat
    partner = lon + sigma
    lop = lat + tau
    xn = lax.rem(lat - tau + 8, 8)
    has_xn = (lat > 0) & (lat < 7)
    no_xn = (lat == 0) | (lat == 7)
    depth = lon // 2
    up, down = lax.rem(lon + 2, 16), lax.rem(lon + 14, 16)
    zp = lax.rem(lon + 2 * sigma + 16, 16)
    zm = lax.rem(lon - 2 * sigma + 16, 16)
    other = 1 - lev
    far, opp = 3 + odd_lon, 4 - odd_lon
    prow, xrow = 3 * (1 - odd_lat), 3 * odd_lat

    def device(lo=None, la=None, le=None):
        return (lon if lo is None else lo, lat if la is None else la, lev if le is None else le)

    last = depth == 7
    first = depth == 0
    wraps = lon == 15
    wrapped, wrapped_edges = lon == 0, lon == 1
    sends_near = (depth < 7) | (odd_lon == 1)
    sends_edges = (depth < 7) | (odd_lon == 0)
    takes_near = (depth > 0) | (odd_lon == 1)
    takes_edges = (depth > 0) | (odd_lon == 0)
    barrier = pltpu.get_barrier_semaphore()

    def greet(peer):
        pl.semaphore_signal(barrier, inc=1, device_id=peer, device_id_type=MESH)

    even_lon, even_lat = odd_lon == 0, odd_lat == 0
    beside = [
        (device(lo=partner), even_lon, None),
        (device(la=lop), even_lat, None),
        (device(la=xn), odd_lat == 1, has_xn),
        (device(lo=partner, la=lop), even_lon, None),
        (device(lo=partner, la=xn), even_lon, has_xn),
        (device(le=other), lev == 0, None),
    ]
    greetings = jnp.where(first, 0, 1) + jnp.where(last, 1, 0)
    for peer, greets, exists in beside:
        greetings += jnp.where(greets, 0, 1 if exists is None else jnp.where(exists, 1, 0))

        @pl.when(greets if exists is None else greets & exists)
        def _():
            greet(peer)

    @pl.when(depth < 7)
    def _():
        greet(device(lo=up))

    @pl.when(first)
    def _():
        greet(device(lo=down))

    @pl.when(wrapped)
    def _():
        greet(device(lo=15))

    loads = []
    for r in range(2):
        loads.append(pltpu.make_async_copy(tokens.at[:, r], win.at[0, 1 + r], local.at[r]))
    loads.append(pltpu.make_async_copy(w_qkv, v_qkv, local.at[2]))
    loads.append(pltpu.make_async_copy(w_out, v_out, local.at[3]))
    loads.append(pltpu.make_async_copy(w_up, v_up, local.at[4]))
    loads.append(pltpu.make_async_copy(w_down, v_down, local.at[5]))
    for load in loads[:3]:
        load.start()
    tables = [
        pltpu.make_async_copy(tile_mask_h, tile_mask, local.at[6]),
        pltpu.make_async_copy(level_group_h, level_group, local.at[7]),
        pltpu.make_async_copy(row_shift_h, row_shift, local.at[8]),
    ]
    for table in tables:
        table.start()

    greetings += jnp.where(wraps, 1, 0)
    @pl.when(greetings > 0)
    def _():
        pl.semaphore_wait(barrier, greetings)

    for number, (peer, greets, exists) in enumerate(beside):
        answers = jnp.logical_not(greets)

        @pl.when(answers if exists is None else answers & exists)
        def _():
            pl.semaphore_signal(ready.at[2 + number], inc=1, device_id=peer, device_id_type=MESH)

    def await_peer(*numbers):
        for number in numbers:
            _, greets, exists = beside[number]

            @pl.when(greets if exists is None else greets & exists)
            def _():
                pl.semaphore_wait(ready.at[2 + number], 1)

    @pl.when(depth > 0)
    def _():
        pl.semaphore_signal(ready.at[0], inc=1, device_id=device(lo=down), device_id_type=MESH)

    @pl.when(last)
    def _():
        pl.semaphore_signal(ready.at[1], inc=1, device_id=device(lo=up), device_id_type=MESH)

    up_row, down_row = 1 - odd_lat, odd_lat
    lop_at, xn_at = 3 * odd_lat, 3 * (1 - odd_lat)
    routes = {
        M_LOP: (tokens.at[:, up_row], win.at[0, lop_at], device(la=lop)),
        M_XN: (tokens.at[:, down_row], win.at[0, xn_at], device(la=xn)),
        M_PLOP: (tokens.at[:, up_row], win.at[1, lop_at], device(lo=partner, la=lop)),
        M_PXN: (tokens.at[:, down_row], win.at[1, xn_at], device(lo=partner, la=xn)),
        M_OPP + 2: (win.at[0, prow], win.at[opp, prow], device(lo=zm)),
        M_OPP + 3: (win.at[0, xrow], win.at[opp, xrow], device(lo=zm)),
        M_FAR_LOP: (win.at[far, 1 + up_row], win.at[far, lop_at], device(la=lop)),
        M_FAR_XN: (win.at[far, 1 + down_row], win.at[far, xn_at], device(la=xn)),
        M_OPP_LOP: (win.at[opp, 1 + up_row], win.at[opp, lop_at], device(la=lop)),
        M_OPP_XN: (win.at[opp, 1 + down_row], win.at[opp, xn_at], device(la=xn)),
        M_OPP_PLOP: (
            win.at[opp, 1 + up_row], win.at[2, lop_at], device(lo=partner, la=lop)),
        M_OPP_PXN: (
            win.at[opp, 1 + down_row], win.at[2, xn_at], device(lo=partner, la=xn)),
    }
    for r in range(2):
        routes[M_PARTNER + r] = (tokens.at[:, r], win.at[1, 1 + r], device(lo=partner))
        routes[M_FAR + r] = (tokens.at[:, r], win.at[far, 1 + r], device(lo=zp))
        routes[M_OPP + r] = (tokens.at[:, r], win.at[opp, 1 + r], device(lo=zm))
        routes[M_NEAR + r] = (win.at[1, 1 + r], win.at[2, 1 + r], device(lo=zp))
        routes[M_WRAP + r] = (tokens.at[:, r], win.at[2, 1 + r], device(lo=0))
        routes[M_SIB + r] = (tokens.at[:, r], sib.at[r], device(le=other))
        routes[M_PART + r] = (part.at[r], got.at[r], device(le=other))
    def message(number):
        src, dst, peer = routes[number]
        return pltpu.make_async_remote_copy(
            src_ref=src, dst_ref=dst, send_sem=send.at[number], recv_sem=recv.at[number],
            device_id=peer, device_id_type=MESH,
        )

    def begin(*numbers):
        for number in numbers:
            message(number).start()

    def arrived(*numbers):
        for number in numbers:
            message(number).wait_recv()

    zp_step = jnp.where(odd_lon == 0, jnp.where(last, 0, 1), jnp.where(first, 2, 0))
    zm_step = jnp.where(odd_lon == 1, jnp.where(last, 0, 1), jnp.where(first, 2, 0))

    def begin_z(step):
        @pl.when(zp_step == step)
        def _():
            begin(M_FAR, M_FAR + 1)

        @pl.when(zm_step == step)
        def _():
            begin(M_OPP, M_OPP + 1)

    begin_z(0)

    await_peer(0)
    begin(M_PARTNER + 1)

    @pl.when(wraps)
    def _():
        begin(M_WRAP)

    begin(M_PARTNER)
    await_peer(5)
    begin(M_SIB, M_SIB + 1)

    @pl.when(depth < 7)
    def _():
        pl.semaphore_wait(ready.at[0], 1)

    begin_z(1)
    await_peer(1, 3, 2, 4)
    begin(M_LOP, M_PLOP)

    @pl.when(has_xn)
    def _():
        begin(M_XN, M_PXN)

    for load in loads[3:]:
        load.start()

    @pl.when(no_xn)
    def _():
        for slot in range(5):
            win[slot, xrow] = jnp.zeros((4, 16, WIDTH), BF16)

    def project_queries(owner, rows):
        normed = normalize(rows.astype(F32)).astype(BF16)
        q = jnp.dot(normed, v_qkv[:, :WIDTH], preferred_element_type=F32) * HEAD_DIM ** (-0.5)
        queries[owner] = q.astype(BF16).reshape(2, 64, WIDTH)

    def project(pieces):
        rows = jnp.concatenate([piece.reshape(64, WIDTH) for piece in pieces], axis=0)
        normed = normalize(rows.astype(F32)).astype(BF16)
        both = jnp.dot(normed, v_qkv[:, WIDTH:], preferred_element_type=F32).astype(BF16)
        return [both[64 * i:64 * (i + 1)] for i in range(len(pieces))]

    def project_keys(places):
        for (slot, row), piece in zip(places, project([win[place] for place in places])):
            kv[slot, row] = piece

    for load in loads[:3]:
        load.wait()
    project_queries(1, win[0, 1:3].reshape(128, WIDTH))

    project_keys([(0, 1), (0, 2)])

    for table in tables:
        table.wait()

    def iota(shape, dim):
        return lax.broadcasted_iota(jnp.int32, shape, dim)

    def spread(at, starts, values):
        result = jnp.full(at.shape, values[0], jnp.int32)
        for start, value in zip(starts[1:], values[1:]):
            result = jnp.where(at >= start, value, result)
        return result

    own_at = iota((64, 1), 0)
    q_col = own_at & 15
    q_lev = lax.shift_right_logical(own_at, 4)

    def pick(index, values):
        result = jnp.full(index.shape, values[0], jnp.int32)
        for i in range(1, len(values)):
            result = jnp.where(index == i, values[i], result)
        return result

    own_groups = [level_group[lev * 4 + i] for i in range(4)]
    q_groups = [
        pick(q_lev, [level_group[whose * 4 + i] for i in range(4)]) for whose in (other, lev)]
    dyn_slot = []
    for r in range(2):
        shift = row_shift[r]
        right = shift > 0
        dyn_slot.append(jnp.where(right, 4, 3))
        dyn_offset = jnp.where(right, 2, -2)
        dyn_ok = jnp.where(right, tile_mask[0, 0, 4], tile_mask[0, 0, 0])
        west, east = tile_mask[0, 0, 1], tile_mask[0, 0, 3]
        near_ok = jnp.where(odd_lon == 0, west, east)
        partner_ok = jnp.where(odd_lon == 0, east, west)
        edge = 3 * r
        for mask, starts, first_rows, offsets, tiles in (
            (bias, (0, 192, 384), (r, r, 1), (0, sigma, dyn_offset), (1, partner_ok, dyn_ok)),
            (bias_far, (0, 192), (r, edge), (-sigma, dyn_offset), (near_ok, dyn_ok)),
        ):
            at = iota((1, mask.shape[-1]), 1)
            in_segment = at - spread(at, starts, starts)
            key_row = lax.shift_right_logical(in_segment, 6) + spread(at, starts, first_rows)
            key_lev = lax.shift_right_logical(in_segment & 63, 4)
            key_col = in_segment & 15
            absolute = lat * 2 - 1 + key_row
            row_ok = (absolute >= 0) & (absolute < 16)
            offset = spread(at, starts, offsets)
            tile_ok = spread(at, starts, tiles)
            distance = offset * 16 + key_col - q_col
            near = (jnp.abs(distance) <= 8) | (jnp.abs(distance - shift) <= 8)
            near = near & (row_ok & (tile_ok > 0))
            key_group = pick(key_lev, own_groups)
            for owner in range(2):
                visible = near & (q_groups[owner] == key_group)
                mask[owner, r] = jnp.where(visible, 0.0, -jnp.inf).astype(F32)

    def forward_near(r):
        pl.when(sends_near | (r == 1))(lambda: begin(M_NEAR + r))

    def forward_edges():
        @pl.when(sends_edges)
        def _():
            begin(M_OPP + 2)

            @pl.when(has_xn)
            def _():
                begin(M_OPP + 3)

    def forward_far():
        arrived(M_FAR, M_FAR + 1)
        begin(M_FAR_LOP)

        @pl.when(has_xn)
        def _():
            begin(M_FAR_XN)

    def forward_opp():
        arrived(M_OPP, M_OPP + 1)

        @pl.when(wrapped_edges)
        def _():
            begin(M_OPP_LOP)

            @pl.when(has_xn)
            def _():
                begin(M_OPP_XN)

        begin(M_OPP_PLOP)

        @pl.when(has_xn)
        def _():
            begin(M_OPP_PXN)

    def project_far():
        project_keys([(slot, row) for slot in (3, 4) for row in (1, 2)])

    @pl.when(first)
    def _():
        pl.semaphore_wait(ready.at[1], 1)

    begin_z(2)
    arrived(M_PARTNER + 1)
    forward_near(1)
    arrived(M_PARTNER)
    forward_near(0)
    arrived(M_LOP)

    @pl.when(has_xn)
    def _():
        arrived(M_XN)

    forward_edges()
    arrived(M_SIB, M_SIB + 1)
    project_queries(0, sib[...].reshape(128, WIDTH))

    pl.when(lon != 0)(forward_far)
    pl.when(lon != 1)(forward_opp)
    pl.when(depth > 0)(project_far)

    pl.when(lon == 0)(forward_far)
    pl.when(lon == 1)(forward_opp)
    arrived(M_PLOP)

    @pl.when(has_xn)
    def _():
        arrived(M_PXN)

    project_keys([(1, row) for row in range(4)] + [(0, 0), (0, 3)])


    pl.when(first)(project_far)

    lane_head = lax.shift_right_logical(iota((1, HALF), 1), 5)
    head_is = [lane_head == h for h in range(8)]
    head_one = [h.astype(F32).astype(BF16) for h in head_is]

    def attend(owner, r, half, phase, mask):
        lower = half * HALF
        q = queries[owner, r, :, lower:lower + HALF]
        stacked = jnp.concatenate([q * head_one[h] for h in range(8)], axis=0)
        def gather(start):
            lanes = slice(start, start + HALF)
            pieces = [kv[slot, r:r + 3, :, lanes] for slot in ((0, 1) if phase == 0 else (2,))]
            pieces.append(kv[dyn_slot[r], 1:3, :, lanes] if phase == 0 else kv_edge[r, :, lanes])
            return jnp.concatenate([piece.reshape(-1, HALF) for piece in pieces], axis=0)

        k, v = gather(lower), gather(WIDTH + lower)
        scores = lax.dot_general(
            stacked, k, (((1,), (1,)), ((), ())), preferred_element_type=F32)
        scores = scores.reshape(8, 64, -1) + mask[owner, r][None]
        highest = jnp.maximum(jnp.max(scores, axis=-1, keepdims=True), EMPTY)
        weights = jnp.exp(scores - highest)
        total = jnp.sum(weights, axis=-1, keepdims=True)
        probs = weights.astype(BF16).reshape(512, -1)
        summed = jnp.dot(probs, v, preferred_element_type=F32).reshape(8, 64, HALF)
        o, m, l = summed[0], highest[0], total[0]
        for h in range(1, 8):
            o = jnp.where(head_is[h], summed[h], o)
            m = jnp.where(head_is[h], highest[h], m)
            l = jnp.where(head_is[h], total[h], l)
        return o, m, l

    for owner in range(2):
        for r in range(2):
            for half in range(2):
                o, m, l = attend(owner, r, half, 0, bias)
                at = (owner, r, slice(None), slice(half * HALF, (half + 1) * HALF))
                keep_o[at], keep_m[at], keep_l[at] = o, m, l

    arrived(M_NEAR + 1)

    @pl.when(takes_near)
    def _():
        arrived(M_NEAR)

    @pl.when(wrapped)
    def _():
        arrived(M_WRAP)

    project_keys([(2, 1), (2, 2)])

    def merged(owner, r, half, phase, mask):
        o, m, l = attend(owner, r, half, phase, mask)
        at = (owner, r, slice(None), slice(half * HALF, (half + 1) * HALF))
        top = jnp.maximum(m, keep_m[at])
        old, new = jnp.exp(keep_m[at] - top), jnp.exp(m - top)
        return at, old * keep_o[at] + new * o, top, old * keep_l[at] + new * l

    @pl.when(takes_edges)
    def _():
        arrived(M_OPP + 2)

        @pl.when(has_xn)
        def _():
            arrived(M_OPP + 3)

    @pl.when(wrapped_edges)
    def _():
        arrived(M_OPP_LOP)

        @pl.when(has_xn)
        def _():
            arrived(M_OPP_XN)

    arrived(M_FAR_LOP, M_OPP_PLOP)

    @pl.when(has_xn)
    def _():
        arrived(M_FAR_XN, M_OPP_PXN)

    kv[2, 0], kv[2, 3], kv_edge[0], kv_edge[1] = project(
        [win[2, 0], win[2, 3], win[dyn_slot[0], 0], win[dyn_slot[1], 3]])

    for owner in range(2):
        for r in range(2):
            for half in range(2):
                at, o, top, l = merged(owner, r, half, 1, bias_far)
                l = jnp.maximum(l, TINY)
                if owner == 0:
                    part[r, 0, :, at[-1]] = o / l
                    part[r, 1, :, at[-1]] = top + jnp.log(l)
                else:
                    keep_o[at], keep_m[at] = o / l, top + jnp.log(l)
            if owner == 0:
                begin(M_PART + r)

    rows = []
    for r in range(2):
        arrived(M_PART + r)
        mine, theirs = keep_m[1, r], got[r, 1]
        top = jnp.maximum(mine, theirs)
        mine, theirs = jnp.exp(mine - top), jnp.exp(theirs - top)
        rows.append((mine * keep_o[1, r] + theirs * got[r, 0]) / (mine + theirs))
    attended = jnp.concatenate(rows, axis=0).astype(BF16)

    for load in loads[3:]:
        load.wait()
    inputs = win[0, 1:3].reshape(128, WIDTH).astype(F32)
    middle = inputs + jnp.dot(attended, v_out[...], preferred_element_type=F32)
    mid_normed = normalize(middle).astype(BF16)
    updated = middle
    for start in range(0, FF, 2048):
        hidden = jnp.dot(mid_normed, v_up[:, start:start + 2048], preferred_element_type=F32)
        hidden = 0.5 * hidden * (1.0 + lax.erf(hidden * 0.5 ** 0.5))
        updated = updated + jnp.dot(
            hidden.astype(BF16), v_down[start:start + 2048, :], preferred_element_type=F32)
    updated = updated.astype(BF16).reshape(2, 4, 16, WIDTH)
    for r in range(2):
        out[:, r] = updated[r]

    def sent(*numbers):
        for number in numbers:
            message(number).wait_send()

    sent(*range(M_PARTNER, M_PARTNER + 2), M_LOP, M_PLOP, M_FAR, M_FAR + 1, M_OPP, M_OPP + 1)
    sent(M_FAR_LOP, M_OPP_PLOP, M_SIB, M_SIB + 1, M_PART, M_PART + 1)

    @pl.when(has_xn)
    def _():
        sent(M_XN, M_PXN, M_FAR_XN, M_OPP_PXN)

    @pl.when(sends_near)
    def _():
        sent(M_NEAR)

    sent(M_NEAR + 1)

    @pl.when(sends_edges)
    def _():
        sent(M_OPP + 2)

        @pl.when(has_xn)
        def _():
            sent(M_OPP + 3)

    @pl.when(wraps)
    def _():
        sent(M_WRAP)

    @pl.when(wrapped_edges)
    def _():
        sent(M_OPP_LOP)

        @pl.when(has_xn)
        def _():
            sent(M_OPP_XN)


def on_device(tokens, w_qkv, w_out, w_up, w_down, tile_mask, level_group, row_shift):
    anywhere = pl.BlockSpec(memory_space=pltpu.HBM)
    vmem = pltpu.VMEM
    return pl.pallas_call(
        kernel,
        out_shape=vmem(tokens.shape, BF16),
        in_specs=[anywhere] * 8,
        out_specs=pl.BlockSpec(memory_space=pltpu.VMEM),
        scratch_shapes=[
            pltpu.SMEM((1, 1, 5), jnp.int32),
            pltpu.SMEM((8,), jnp.int32),
            pltpu.SMEM((2,), jnp.int32),
            vmem((5, 4, 4, 16, WIDTH), BF16),
            vmem((2, 4, 16, WIDTH), BF16),
            vmem((WIDTH, 3 * WIDTH), BF16),
            vmem((WIDTH, WIDTH), BF16),
            vmem((WIDTH, FF), BF16),
            vmem((FF, WIDTH), BF16),
            vmem((5, 4, 64, 2 * WIDTH), BF16),
            vmem((2, 64, 2 * WIDTH), BF16),
            vmem((2, 2, 64, WIDTH), BF16),
            vmem((2, 2, 64, 512), F32),
            vmem((2, 2, 64, 256), F32),
            vmem((2, 2, 64, WIDTH), F32),
            vmem((2, 2, 64, WIDTH), F32),
            vmem((2, 2, 64, WIDTH), F32),
            vmem((2, 2, 64, WIDTH), F32),
            vmem((2, 2, 64, WIDTH), F32),
            pltpu.SemaphoreType.DMA((MESSAGES,)),
            pltpu.SemaphoreType.DMA((MESSAGES,)),
            pltpu.SemaphoreType.DMA((9,)),
            pltpu.SemaphoreType.REGULAR((8,)),
        ],
        compiler_params=pltpu.CompilerParams(
            collective_id=0, has_side_effects=True, vmem_limit_bytes=60 * 1024 * 1024),
        cost_estimate=pl.CostEstimate(
            flops=6 * 10 ** 9, bytes_accessed=7 * 10 ** 6, transcendentals=4 * 10 ** 6),
    )(tokens, w_qkv, w_out, w_up, w_down, tile_mask, level_group, row_shift)


def solution(mesh):
    placed = (
        P("lev", "lat", "lon", None), P(), P(), P(), P(), P("lat", "lon", None), P(), P("lat"),
    )
    return jax.shard_map(
        on_device, mesh=mesh, in_specs=placed, out_specs=P("lev", "lat", "lon", None),
        check_vma=False,
    )
```

```python
import functools

import jax
import jax.numpy as jnp
from jax import lax
from jax.experimental import pallas as pl
from jax.experimental.pallas import tpu as pltpu
from jax.sharding import PartitionSpec as P

WIDTH = 512
HALF = 256
HEAD_DIM = 32
FF = 2048
EMPTY = -1e30
TINY = 1e-30
F32 = jnp.float32
BF16 = jnp.bfloat16
MESH = pl.DeviceIdType.MESH

M_PARTNER = 0
M_LOP = 2
M_XN = 3
M_PLOP = 4
M_PXN = 5
M_FAR = 6
M_OPP = 8
M_NEAR = 12
M_FAR_LOP = 14
M_FAR_XN = 15
M_OPP_PLOP = 16
M_OPP_PXN = 17
M_SIB = 18
M_PART = 20
M_WRAP = 22
M_OPP_LOP = 24
M_OPP_XN = 25
MESSAGES = 26


def normalize(values):
    centred = values - jnp.mean(values, axis=-1, keepdims=True)
    spread = jnp.mean(centred * centred, axis=-1, keepdims=True)
    return centred * lax.rsqrt(spread + 1e-05)


def kernel(
    tokens, w_qkv, w_out, w_up, w_down, tile_mask_h, level_group_h, row_shift_h, out,
    tile_mask, level_group, row_shift, win, sib, v_qkv, v_out, v_up, v_down, kv, kv_edge, queries, bias,
    bias_far, keep_o, keep_m,
    keep_l, part, got, send, recv, local, ready,
):
    lon, lat, lev = (lax.axis_index(a) for a in ("lon", "lat", "lev"))
    odd_lon, odd_lat = lax.rem(lon, 2), lax.rem(lat, 2)
    sigma, tau = 1 - 2 * odd_lon, 1 - 2 * odd_lat
    partner = lon + sigma
    lop = lat + tau
    xn = lax.rem(lat - tau + 8, 8)
    has_xn = (lat > 0) & (lat < 7)
    no_xn = (lat == 0) | (lat == 7)
    depth = lon // 2
    up, down = lax.rem(lon + 2, 16), lax.rem(lon + 14, 16)
    zp = lax.rem(lon + 2 * sigma + 16, 16)
    zm = lax.rem(lon - 2 * sigma + 16, 16)
    other = 1 - lev
    far, opp = 3 + odd_lon, 4 - odd_lon
    prow, xrow = 3 * (1 - odd_lat), 3 * odd_lat

    def device(lo=None, la=None, le=None):
        return (lon if lo is None else lo, lat if la is None else la, lev if le is None else le)

    last = depth == 7
    first = depth == 0
    wraps = lon == 15
    wrapped, wrapped_edges = lon == 0, lon == 1
    sends_near = (depth < 7) | (odd_lon == 1)
    sends_edges = (depth < 7) | (odd_lon == 0)
    takes_near = (depth > 0) | (odd_lon == 1)
    takes_edges = (depth > 0) | (odd_lon == 0)
    barrier = pltpu.get_barrier_semaphore()

    def greet(peer):
        pl.semaphore_signal(barrier, inc=1, device_id=peer, device_id_type=MESH)

    even_lon, even_lat = odd_lon == 0, odd_lat == 0
    beside = [
        (device(lo=partner), even_lon, None),
        (device(la=lop), even_lat, None),
        (device(la=xn), odd_lat == 1, has_xn),
        (device(lo=partner, la=lop), even_lon, None),
        (device(lo=partner, la=xn), even_lon, has_xn),
        (device(le=other), lev == 0, None),
    ]
    greetings = jnp.where(first, 0, 1) + jnp.where(last, 1, 0)
    for peer, greets, exists in beside:
        greetings += jnp.where(greets, 0, 1 if exists is None else jnp.where(exists, 1, 0))

        @pl.when(greets if exists is None else greets & exists)
        def _():
            greet(peer)

    @pl.when(depth < 7)
    def _():
        greet(device(lo=up))

    @pl.when(first)
    def _():
        greet(device(lo=down))

    @pl.when(wrapped)
    def _():
        greet(device(lo=15))

    loads = []
    for r in range(2):
        loads.append(pltpu.make_async_copy(tokens.at[:, r], win.at[0, 1 + r], local.at[r]))
    loads.append(pltpu.make_async_copy(w_qkv, v_qkv, local.at[2]))
    loads.append(pltpu.make_async_copy(w_out, v_out, local.at[3]))
    loads.append(pltpu.make_async_copy(w_up, v_up, local.at[4]))
    loads.append(pltpu.make_async_copy(w_down, v_down, local.at[5]))
    for load in loads[:3]:
        load.start()
    tables = [
        pltpu.make_async_copy(tile_mask_h, tile_mask, local.at[6]),
        pltpu.make_async_copy(level_group_h, level_group, local.at[7]),
        pltpu.make_async_copy(row_shift_h, row_shift, local.at[8]),
    ]
    for table in tables:
        table.start()

    greetings += jnp.where(wraps, 1, 0)
    @pl.when(greetings > 0)
    def _():
        pl.semaphore_wait(barrier, greetings)

    for number, (peer, greets, exists) in enumerate(beside):
        answers = jnp.logical_not(greets)

        @pl.when(answers if exists is None else answers & exists)
        def _():
            pl.semaphore_signal(ready.at[2 + number], inc=1, device_id=peer, device_id_type=MESH)

    def await_peer(*numbers):
        for number in numbers:
            _, greets, exists = beside[number]

            @pl.when(greets if exists is None else greets & exists)
            def _():
                pl.semaphore_wait(ready.at[2 + number], 1)

    @pl.when(depth > 0)
    def _():
        pl.semaphore_signal(ready.at[0], inc=1, device_id=device(lo=down), device_id_type=MESH)

    @pl.when(last)
    def _():
        pl.semaphore_signal(ready.at[1], inc=1, device_id=device(lo=up), device_id_type=MESH)

    up_row, down_row = 1 - odd_lat, odd_lat
    lop_at, xn_at = 3 * odd_lat, 3 * (1 - odd_lat)
    routes = {
        M_LOP: (tokens.at[:, up_row], win.at[0, lop_at], device(la=lop)),
        M_XN: (tokens.at[:, down_row], win.at[0, xn_at], device(la=xn)),
        M_PLOP: (tokens.at[:, up_row], win.at[1, lop_at], device(lo=partner, la=lop)),
        M_PXN: (tokens.at[:, down_row], win.at[1, xn_at], device(lo=partner, la=xn)),
        M_OPP + 2: (win.at[0, prow], win.at[opp, prow], device(lo=zm)),
        M_OPP + 3: (win.at[0, xrow], win.at[opp, xrow], device(lo=zm)),
        M_FAR_LOP: (win.at[far, 1 + up_row], win.at[far, lop_at], device(la=lop)),
        M_FAR_XN: (win.at[far, 1 + down_row], win.at[far, xn_at], device(la=xn)),
        M_OPP_LOP: (win.at[opp, 1 + up_row], win.at[opp, lop_at], device(la=lop)),
        M_OPP_XN: (win.at[opp, 1 + down_row], win.at[opp, xn_at], device(la=xn)),
        M_OPP_PLOP: (
            win.at[opp, 1 + up_row], win.at[2, lop_at], device(lo=partner, la=lop)),
        M_OPP_PXN: (
            win.at[opp, 1 + down_row], win.at[2, xn_at], device(lo=partner, la=xn)),
    }
    for r in range(2):
        routes[M_PARTNER + r] = (tokens.at[:, r], win.at[1, 1 + r], device(lo=partner))
        routes[M_FAR + r] = (tokens.at[:, r], win.at[far, 1 + r], device(lo=zp))
        routes[M_OPP + r] = (tokens.at[:, r], win.at[opp, 1 + r], device(lo=zm))
        routes[M_NEAR + r] = (win.at[1, 1 + r], win.at[2, 1 + r], device(lo=zp))
        routes[M_WRAP + r] = (tokens.at[:, r], win.at[2, 1 + r], device(lo=0))
        routes[M_SIB + r] = (tokens.at[:, r], sib.at[r], device(le=other))
        routes[M_PART + r] = (part.at[r], got.at[r], device(le=other))
    def message(number):
        src, dst, peer = routes[number]
        return pltpu.make_async_remote_copy(
            src_ref=src, dst_ref=dst, send_sem=send.at[number], recv_sem=recv.at[number],
            device_id=peer, device_id_type=MESH,
        )

    def begin(*numbers):
        for number in numbers:
            message(number).start()

    def arrived(*numbers):
        for number in numbers:
            message(number).wait_recv()

    zp_step = jnp.where(odd_lon == 0, jnp.where(last, 0, 1), jnp.where(first, 2, 0))
    zm_step = jnp.where(odd_lon == 1, jnp.where(last, 0, 1), jnp.where(first, 2, 0))

    def begin_z(step):
        @pl.when(zp_step == step)
        def _():
            begin(M_FAR, M_FAR + 1)

        @pl.when(zm_step == step)
        def _():
            begin(M_OPP, M_OPP + 1)

    begin_z(0)

    await_peer(0)
    begin(M_PARTNER + 1)

    @pl.when(wraps)
    def _():
        begin(M_WRAP)

    begin(M_PARTNER)
    await_peer(5)
    begin(M_SIB, M_SIB + 1)

    @pl.when(depth < 7)
    def _():
        pl.semaphore_wait(ready.at[0], 1)

    begin_z(1)
    await_peer(1, 3, 2, 4)

    @pl.when(has_xn)
    def _():
        begin(M_XN, M_PXN)

    begin(M_LOP, M_PLOP)

    for load in loads[3:]:
        load.start()

    @pl.when(no_xn)
    def _():
        for slot in range(5):
            win[slot, xrow] = jnp.zeros((4, 16, WIDTH), BF16)

    def project_queries(owner, rows):
        normed = normalize(rows.astype(F32)).astype(BF16)
        q = jnp.dot(normed, v_qkv[:, :WIDTH], preferred_element_type=F32) * HEAD_DIM ** (-0.5)
        queries[owner] = q.astype(BF16).reshape(2, 64, WIDTH)

    def project(pieces):
        rows = jnp.concatenate([piece.reshape(64, WIDTH) for piece in pieces], axis=0)
        normed = normalize(rows.astype(F32)).astype(BF16)
        both = jnp.dot(normed, v_qkv[:, WIDTH:], preferred_element_type=F32).astype(BF16)
        return [both[64 * i:64 * (i + 1)] for i in range(len(pieces))]

    def project_keys(places):
        for (slot, row), piece in zip(places, project([win[place] for place in places])):
            kv[slot, row] = piece

    for load in loads[:3]:
        load.wait()
    project_queries(1, win[0, 1:3].reshape(128, WIDTH))

    project_keys([(0, 1), (0, 2)])

    for table in tables:
        table.wait()

    def iota(shape, dim):
        return lax.broadcasted_iota(jnp.int32, shape, dim)

    def spread(at, starts, values):
        result = jnp.full(at.shape, values[0], jnp.int32)
        for start, value in zip(starts[1:], values[1:]):
            result = jnp.where(at >= start, value, result)
        return result

    own_at = iota((64, 1), 0)
    q_col = own_at & 15
    q_lev = lax.shift_right_logical(own_at, 4)

    def pick(index, values):
        result = jnp.full(index.shape, values[0], jnp.int32)
        for i in range(1, len(values)):
            result = jnp.where(index == i, values[i], result)
        return result

    own_groups = [level_group[lev * 4 + i] for i in range(4)]
    q_groups = [
        pick(q_lev, [level_group[whose * 4 + i] for i in range(4)]) for whose in (other, lev)]
    dyn_slot = []
    for r in range(2):
        shift = row_shift[r]
        right = shift > 0
        dyn_slot.append(jnp.where(right, 4, 3))
        dyn_offset = jnp.where(right, 2, -2)
        dyn_ok = jnp.where(right, tile_mask[0, 0, 4], tile_mask[0, 0, 0])
        west, east = tile_mask[0, 0, 1], tile_mask[0, 0, 3]
        near_ok = jnp.where(odd_lon == 0, west, east)
        partner_ok = jnp.where(odd_lon == 0, east, west)
        edge = 3 * r
        for mask, starts, first_rows, offsets, tiles in (
            (bias, (0, 192, 384), (r, r, 1), (0, sigma, dyn_offset), (1, partner_ok, dyn_ok)),
            (bias_far, (0, 192), (r, edge), (-sigma, dyn_offset), (near_ok, dyn_ok)),
        ):
            at = iota((1, mask.shape[-1]), 1)
            in_segment = at - spread(at, starts, starts)
            key_row = lax.shift_right_logical(in_segment, 6) + spread(at, starts, first_rows)
            key_lev = lax.shift_right_logical(in_segment & 63, 4)
            key_col = in_segment & 15
            absolute = lat * 2 - 1 + key_row
            row_ok = (absolute >= 0) & (absolute < 16)
            offset = spread(at, starts, offsets)
            tile_ok = spread(at, starts, tiles)
            distance = offset * 16 + key_col - q_col
            near = (jnp.abs(distance) <= 8) | (jnp.abs(distance - shift) <= 8)
            near = near & (row_ok & (tile_ok > 0))
            key_group = pick(key_lev, own_groups)
            for owner in range(2):
                visible = near & (q_groups[owner] == key_group)
                mask[owner, r] = jnp.where(visible, 0.0, -jnp.inf).astype(F32)

    def forward_near(r):
        pl.when(sends_near | (r == 1))(lambda: begin(M_NEAR + r))

    def forward_edges():
        @pl.when(sends_edges)
        def _():
            begin(M_OPP + 2)

            @pl.when(has_xn)
            def _():
                begin(M_OPP + 3)

    def forward_far():
        arrived(M_FAR, M_FAR + 1)
        @pl.when(has_xn)
        def _():
            begin(M_FAR_XN)

        begin(M_FAR_LOP)

    def forward_opp():
        arrived(M_OPP, M_OPP + 1)

        @pl.when(has_xn)
        def _():
            pl.when(wrapped_edges)(lambda: begin(M_OPP_XN))
            begin(M_OPP_PXN)

        pl.when(wrapped_edges)(lambda: begin(M_OPP_LOP))
        begin(M_OPP_PLOP)

    def project_far():
        project_keys([(slot, row) for slot in (3, 4) for row in (1, 2)])

    @pl.when(first)
    def _():
        pl.semaphore_wait(ready.at[1], 1)

    begin_z(2)
    arrived(M_PARTNER + 1)
    forward_near(1)
    arrived(M_PARTNER)
    forward_near(0)
    arrived(M_LOP)

    @pl.when(has_xn)
    def _():
        arrived(M_XN)

    forward_edges()
    arrived(M_SIB, M_SIB + 1)
    project_queries(0, sib[...].reshape(128, WIDTH))

    pl.when(lon != 0)(forward_far)
    pl.when(lon != 1)(forward_opp)
    pl.when(depth > 0)(project_far)

    pl.when(lon == 0)(forward_far)
    pl.when(lon == 1)(forward_opp)
    arrived(M_PLOP)

    @pl.when(has_xn)
    def _():
        arrived(M_PXN)

    project_keys([(1, row) for row in range(4)] + [(0, 0), (0, 3)])


    pl.when(first)(project_far)

    lane_head = lax.shift_right_logical(iota((1, HALF), 1), 5)
    head_is = [lane_head == h for h in range(8)]
    head_one = [h.astype(F32).astype(BF16) for h in head_is]

    def attend(owner, r, half, phase, mask):
        lower = half * HALF
        q = queries[owner, r, :, lower:lower + HALF]
        stacked = jnp.concatenate([q * head_one[h] for h in range(8)], axis=0)
        def gather(start):
            lanes = slice(start, start + HALF)
            pieces = [kv[slot, r:r + 3, :, lanes] for slot in ((0, 1) if phase == 0 else (2,))]
            pieces.append(kv[dyn_slot[r], 1:3, :, lanes] if phase == 0 else kv_edge[r, :, lanes])
            return jnp.concatenate([piece.reshape(-1, HALF) for piece in pieces], axis=0)

        k, v = gather(lower), gather(WIDTH + lower)
        scores = lax.dot_general(
            stacked, k, (((1,), (1,)), ((), ())), preferred_element_type=F32)
        scores = scores.reshape(8, 64, -1) + mask[owner, r][None]
        highest = jnp.maximum(jnp.max(scores, axis=-1, keepdims=True), EMPTY)
        weights = jnp.exp(scores - highest)
        total = jnp.sum(weights, axis=-1, keepdims=True)
        probs = weights.astype(BF16).reshape(512, -1)
        summed = jnp.dot(probs, v, preferred_element_type=F32).reshape(8, 64, HALF)
        o, m, l = summed[0], highest[0], total[0]
        for h in range(1, 8):
            o = jnp.where(head_is[h], summed[h], o)
            m = jnp.where(head_is[h], highest[h], m)
            l = jnp.where(head_is[h], total[h], l)
        return o, m, l

    for owner in range(2):
        for r in range(2):
            for half in range(2):
                o, m, l = attend(owner, r, half, 0, bias)
                at = (owner, r, slice(None), slice(half * HALF, (half + 1) * HALF))
                keep_o[at], keep_m[at], keep_l[at] = o, m, l

    arrived(M_NEAR + 1)

    @pl.when(takes_near)
    def _():
        arrived(M_NEAR)

    @pl.when(wrapped)
    def _():
        arrived(M_WRAP)

    project_keys([(2, 1), (2, 2)])

    def merged(owner, r, half, phase, mask):
        o, m, l = attend(owner, r, half, phase, mask)
        at = (owner, r, slice(None), slice(half * HALF, (half + 1) * HALF))
        top = jnp.maximum(m, keep_m[at])
        old, new = jnp.exp(keep_m[at] - top), jnp.exp(m - top)
        return at, old * keep_o[at] + new * o, top, old * keep_l[at] + new * l

    @pl.when(takes_edges)
    def _():
        arrived(M_OPP + 2)

        @pl.when(has_xn)
        def _():
            arrived(M_OPP + 3)

    @pl.when(wrapped_edges)
    def _():
        arrived(M_OPP_LOP)

        @pl.when(has_xn)
        def _():
            arrived(M_OPP_XN)

    arrived(M_FAR_LOP, M_OPP_PLOP)

    @pl.when(has_xn)
    def _():
        arrived(M_FAR_XN, M_OPP_PXN)

    kv[2, 0], kv[2, 3], kv_edge[0], kv_edge[1] = project(
        [win[2, 0], win[2, 3], win[dyn_slot[0], 0], win[dyn_slot[1], 3]])

    for owner in range(2):
        for r in range(2):
            for half in range(2):
                at, o, top, l = merged(owner, r, half, 1, bias_far)
                l = jnp.maximum(l, TINY)
                if owner == 0:
                    part[r, 0, :, at[-1]] = o / l
                    part[r, 1, :, at[-1]] = top + jnp.log(l)
                else:
                    keep_o[at], keep_m[at] = o / l, top + jnp.log(l)
            if owner == 0:
                begin(M_PART + r)

    rows = []
    for r in range(2):
        arrived(M_PART + r)
        mine, theirs = keep_m[1, r], got[r, 1]
        top = jnp.maximum(mine, theirs)
        mine, theirs = jnp.exp(mine - top), jnp.exp(theirs - top)
        rows.append((mine * keep_o[1, r] + theirs * got[r, 0]) / (mine + theirs))
    attended = jnp.concatenate(rows, axis=0).astype(BF16)

    for load in loads[3:]:
        load.wait()
    inputs = win[0, 1:3].reshape(128, WIDTH).astype(F32)
    middle = inputs + jnp.dot(attended, v_out[...], preferred_element_type=F32)
    mid_normed = normalize(middle).astype(BF16)
    updated = middle
    for start in range(0, FF, 2048):
        hidden = jnp.dot(mid_normed, v_up[:, start:start + 2048], preferred_element_type=F32)
        hidden = 0.5 * hidden * (1.0 + lax.erf(hidden * 0.5 ** 0.5))
        updated = updated + jnp.dot(
            hidden.astype(BF16), v_down[start:start + 2048, :], preferred_element_type=F32)
    updated = updated.astype(BF16).reshape(2, 4, 16, WIDTH)
    for r in range(2):
        out[:, r] = updated[r]

    def sent(*numbers):
        for number in numbers:
            message(number).wait_send()

    sent(*range(M_PARTNER, M_PARTNER + 2), M_LOP, M_PLOP, M_FAR, M_FAR + 1, M_OPP, M_OPP + 1)
    sent(M_FAR_LOP, M_OPP_PLOP, M_SIB, M_SIB + 1, M_PART, M_PART + 1)

    @pl.when(has_xn)
    def _():
        sent(M_XN, M_PXN, M_FAR_XN, M_OPP_PXN)

    @pl.when(sends_near)
    def _():
        sent(M_NEAR)

    sent(M_NEAR + 1)

    @pl.when(sends_edges)
    def _():
        sent(M_OPP + 2)

        @pl.when(has_xn)
        def _():
            sent(M_OPP + 3)

    @pl.when(wraps)
    def _():
        sent(M_WRAP)

    @pl.when(wrapped_edges)
    def _():
        sent(M_OPP_LOP)

        @pl.when(has_xn)
        def _():
            sent(M_OPP_XN)


def on_device(tokens, w_qkv, w_out, w_up, w_down, tile_mask, level_group, row_shift):
    anywhere = pl.BlockSpec(memory_space=pltpu.HBM)
    vmem = pltpu.VMEM
    return pl.pallas_call(
        kernel,
        out_shape=vmem(tokens.shape, BF16),
        in_specs=[anywhere] * 8,
        out_specs=pl.BlockSpec(memory_space=pltpu.VMEM),
        scratch_shapes=[
            pltpu.SMEM((1, 1, 5), jnp.int32),
            pltpu.SMEM((8,), jnp.int32),
            pltpu.SMEM((2,), jnp.int32),
            vmem((5, 4, 4, 16, WIDTH), BF16),
            vmem((2, 4, 16, WIDTH), BF16),
            vmem((WIDTH, 3 * WIDTH), BF16),
            vmem((WIDTH, WIDTH), BF16),
            vmem((WIDTH, FF), BF16),
            vmem((FF, WIDTH), BF16),
            vmem((5, 4, 64, 2 * WIDTH), BF16),
            vmem((2, 64, 2 * WIDTH), BF16),
            vmem((2, 2, 64, WIDTH), BF16),
            vmem((2, 2, 64, 512), F32),
            vmem((2, 2, 64, 256), F32),
            vmem((2, 2, 64, WIDTH), F32),
            vmem((2, 2, 64, WIDTH), F32),
            vmem((2, 2, 64, WIDTH), F32),
            vmem((2, 2, 64, WIDTH), F32),
            vmem((2, 2, 64, WIDTH), F32),
            pltpu.SemaphoreType.DMA((MESSAGES,)),
            pltpu.SemaphoreType.DMA((MESSAGES,)),
            pltpu.SemaphoreType.DMA((9,)),
            pltpu.SemaphoreType.REGULAR((8,)),
        ],
        compiler_params=pltpu.CompilerParams(
            collective_id=0, has_side_effects=True, vmem_limit_bytes=60 * 1024 * 1024),
        cost_estimate=pl.CostEstimate(
            flops=6 * 10 ** 9, bytes_accessed=7 * 10 ** 6, transcendentals=4 * 10 ** 6),
    )(tokens, w_qkv, w_out, w_up, w_down, tile_mask, level_group, row_shift)


def solution(mesh):
    placed = (
        P("lev", "lat", "lon", None), P(), P(), P(), P(), P("lat", "lon", None), P(), P("lat"),
    )
    return jax.shard_map(
        on_device, mesh=mesh, in_specs=placed, out_specs=P("lev", "lat", "lon", None),
        check_vma=False,
    )
```
